32 devices in a mesh: grp: 2 (over y), tok: 4 (over x, core), feat: 4 (over z).
Axes of the slice: x: 2, y: 2, z: 4, core: 2. Of those that a mesh axis runs over, the one named last changes fastest.
Arguments:
- query_matrix_rows: bfloat16 [2048, 32, 128], P(('grp', 'tok'), 'feat'), parts along dimension 0, may hold values from -1.796875 to 1.796875
- key_matrix_rows: bfloat16 [2048, 2, 128], P(('grp', 'tok')), parts along dimension 0, may hold values from -1.796875 to 1.796875
- value_rows: bfloat16 [2048, 2, 128], P(('grp', 'tok')), parts along dimension 0, may hold values from -40 to 40
- incoming_state: float32 [4, 16384, 128], P('grp', 'feat'), parts along dimension 0, may hold values from -14 to 14
- out_gain: float32 [128], replicated, may hold values from 0.1 to 1.9
Outputs:
- attended: bfloat16 [2048, 32, 128], P(('grp', 'tok'), 'feat'), parts along dimension 0
The draws below stay inside these ranges and needn't reach their ends.
There are 2 independent parts, one for each index of `grp`. The reference program is written for one: setup_inputs(seed, part) draws one part's arguments, and reference() takes and returns one part's arrays. A program takes and returns all parts, laid end to end along the dimension named above; an argument that names none is the same for every part. Nothing has to cross between parts.
All inputs are finite; a program needn't handle non-finite values.
Results may differ from the reference program's by a relative error of at most 0.0033.
Values may be sent and summed in bfloat16 or wider, within the bound.
A program may use at most 192 MiB of HBM per device.

```python
import math
import jax
import jax.numpy as jnp
from jax import lax

HEAD_SIZE = 128
QUERY_HEAD_COUNT = 32
KEY_VALUE_HEADS = 2
BLOCK_TOKENS = 256
WINDOW_TOKENS = 1024
FEATS = 16384
N_TOK = 4


def draw_value_rows(key, part):
    leading_key, second_key, trailing_key = jax.random.split(key, 3)
    normalizer_share = jnp.clip(jax.random.normal(leading_key, (WINDOW_TOKENS, KEY_VALUE_HEADS, HEAD_SIZE), jnp.float32), -4.0, 4.0)
    token_scale = jnp.exp(jax.random.uniform(second_key, (WINDOW_TOKENS, 1, 1), jnp.float32, 0.0, math.log(10.0)))
    channel_factor = jnp.exp(jax.random.uniform(trailing_key, (1, KEY_VALUE_HEADS, HEAD_SIZE), jnp.float32, 0.0, math.log(10.0)))
    return (0.1 * normalizer_share * token_scale * channel_factor).astype(jnp.bfloat16)


def steps_of(own_key, dims, shards, smallest, high):
    gain = 1.0
    for dim, shards_of in shards:
        heights = jax.random.uniform(jax.random.fold_in(jax.random.fold_in(own_key, 6), dim), (shards_of,), jnp.float32, smallest / len(shards), high / len(shards))
        gain = gain * jnp.repeat(jnp.exp(heights), dims[dim] // shards_of).reshape((-1,) + (1,) * (len(dims) - 1 - dim))
    return gain


def noise(stream_key, extent, spread, most, cuts=(), kind=jnp.bfloat16):
    entries = jax.random.normal(stream_key, extent, jnp.float32) * spread
    if len(cuts) > 0:
        entries = steps_of(stream_key, extent, cuts, -0.22, 0.18) * entries
    return jnp.clip(entries, min=-most, max=most).astype(kind)


def setup_inputs(seed: int = 0, part: int = 0) -> dict:
    seeds = jax.random.split(jax.random.key(seed), 6)
    own_keys = jax.random.split(jax.random.fold_in(seeds[5], part), 6)
    query_matrix_rows = noise(own_keys[0], (WINDOW_TOKENS, QUERY_HEAD_COUNT, HEAD_SIZE), 0.3, 1.796875, ((0, 4), (1, 4)))
    key_matrix_rows = noise(own_keys[1], (WINDOW_TOKENS, KEY_VALUE_HEADS, HEAD_SIZE), 0.3, 1.796875, ((0, 4),))
    value_rows = draw_value_rows(jax.random.fold_in(jax.random.fold_in(seeds[5], part), 71), part)
    incoming_state = noise(own_keys[3], (KEY_VALUE_HEADS, FEATS, HEAD_SIZE), (0.1 * (WINDOW_TOKENS // 2) ** 0.5), 14.0, ((1, 4),), jnp.float32)
    out_gain = jnp.clip(1.0 + 0.18 * jax.random.normal(seeds[4], (HEAD_SIZE,), jnp.float32), 0.1, 1.9)
    return dict(query_matrix_rows=query_matrix_rows, key_matrix_rows=key_matrix_rows, value_rows=value_rows, incoming_state=incoming_state, out_gain=out_gain)


def reference(query_matrix_rows, key_matrix_rows, value_rows, incoming_state, out_gain):
    group_count = QUERY_HEAD_COUNT // KEY_VALUE_HEADS
    query_float = query_matrix_rows.astype(jnp.float32).reshape(N_TOK, BLOCK_TOKENS, KEY_VALUE_HEADS, group_count, HEAD_SIZE)
    key_f = key_matrix_rows.astype(jnp.float32)
    value_f = value_rows.astype(jnp.float32)
    causal_mask = jnp.arange(BLOCK_TOKENS)[:, None] >= jnp.arange(BLOCK_TOKENS)[None, :]
    token_ids = jnp.arange(WINDOW_TOKENS, dtype=jnp.int32)
    sub_rows = 8
    sub_count = BLOCK_TOKENS // sub_rows

    def one_block(block_id):
        block_id = jnp.asarray(block_id).astype(jnp.int32)
        queries = lax.dynamic_index_in_dim(query_float, block_id, 0, keepdims=False)
        first_row = block_id * BLOCK_TOKENS
        keys_now = lax.dynamic_slice_in_dim(key_f, first_row, BLOCK_TOKENS, 0)
        values_now = lax.dynamic_slice_in_dim(value_f, first_row, BLOCK_TOKENS, 0)
        all_scores = jnp.einsum('tgrd,ugd->grtu', queries, key_f, precision=lax.Precision.HIGHEST)
        earlier = (token_ids < first_row)[None, None, None, :]
        far_weights = jnp.where(earlier, all_scores * all_scores, 0.0)
        carried = jnp.einsum('grtu,uge->tgre', far_weights, value_f, precision=lax.Precision.HIGHEST)

        def state_read(sub_id):
            sub_id = jnp.asarray(sub_id).astype(jnp.int32)
            picked = lax.dynamic_slice_in_dim(queries, sub_id * sub_rows, sub_rows, 0)
            phi_query = (picked[..., :, None] * picked[..., None, :]).reshape(sub_rows, KEY_VALUE_HEADS, group_count, HEAD_SIZE * HEAD_SIZE)
            return jnp.einsum('tgrf,gfe->tgre', phi_query, incoming_state, precision=lax.Precision.HIGHEST)
        from_state = lax.map(state_read, jnp.arange(sub_count, dtype=jnp.int32))
        carried = carried + from_state.reshape(BLOCK_TOKENS, KEY_VALUE_HEADS, group_count, HEAD_SIZE)
        scores = jnp.einsum('tgrd,ugd->grtu', queries, keys_now, precision=lax.Precision.HIGHEST)
        weights = jnp.where(causal_mask, scores * scores, 0.0)
        weights = lax.optimization_barrier(weights.astype(jnp.bfloat16)).astype(jnp.float32)
        local_read = jnp.einsum('grtu,uge->tgre', weights, values_now, precision=lax.Precision.HIGHEST)
        summed = (local_read + carried).reshape(BLOCK_TOKENS, QUERY_HEAD_COUNT, HEAD_SIZE)
        mean_square = lax.optimization_barrier(jnp.mean(summed * summed, axis=-1, keepdims=True))
        return (summed * lax.rsqrt(mean_square + 1e-06) * out_gain).astype(jnp.bfloat16)
    outputs = lax.map(one_block, jnp.arange(N_TOK, dtype=jnp.int32))
    return outputs.reshape(WINDOW_TOKENS, QUERY_HEAD_COUNT, HEAD_SIZE)
```

```python
import functools

import jax
import jax.numpy as jnp
from jax import lax
from jax.experimental import pallas as pl
from jax.experimental.pallas import tpu as pltpu
from jax.sharding import PartitionSpec as P

QUERY_HEAD_COUNT = 32
KEY_VALUE_HEADS = 2
MESH = pl.DeviceIdType.MESH


def flip(place, bit):
    return place + bit - 2 * bit * ((place // bit) % 2)


def kernel(
    n_feat, n_tok, heads_dev, row_tile,
    q_ref, kv_ref, state_ref, gain_ref, out_ref,
    state_all, send_buf, kv_all, acc,
    z_send, z_recv, f_send, f_recv, kv_send, kv_recv,
):
    z = lax.axis_index("feat")
    t = lax.axis_index("tok")
    group = QUERY_HEAD_COUNT // KEY_VALUE_HEADS
    rows, head = q_ref.shape
    slice_len = state_all.shape[1]
    slice_rows = slice_len // head
    piece = slice_len // n_tok
    tiles = rows // row_tile
    keys = kv_ref.shape[1]
    bits = []
    while 2 ** len(bits) < n_tok:
        bits.append(n_tok // 2 ** (len(bits) + 1))

    barrier = pltpu.get_barrier_semaphore()
    for step in range(1, n_feat):
        pl.semaphore_signal(
            barrier, inc=1, device_id={"feat": lax.rem(z + step, n_feat)}, device_id_type=MESH
        )
    for step in range(1, n_tok):
        pl.semaphore_signal(
            barrier, inc=1, device_id={"tok": lax.rem(t + step, n_tok)}, device_id_type=MESH
        )

    first = pl.multiple_of(t * piece, piece)
    for g in range(KEY_VALUE_HEADS):
        send_buf[g] = state_ref[g, pl.ds(first, piece), :].astype(jnp.bfloat16)

    pl.semaphore_wait(barrier, n_feat + n_tok - 2)

    pending = []
    z_copies = []
    for step in range(1, n_feat):
        peer = lax.rem(z + step, n_feat)
        copy = pltpu.make_async_remote_copy(
            src_ref=send_buf.at[peer * heads_dev // group],
            dst_ref=state_all.at[z, pl.ds(first, piece), :],
            send_sem=z_send.at[step - 1],
            recv_sem=z_recv.at[step - 1],
            device_id={"feat": peer},
            device_id_type=MESH,
        )
        copy.start()
        pending.append(copy)
        z_copies.append(copy)
    kv_copies = []
    for step in range(1, n_tok):
        copy = pltpu.make_async_remote_copy(
            src_ref=kv_ref,
            dst_ref=kv_all.at[t],
            send_sem=kv_send.at[step - 1],
            recv_sem=kv_recv.at[step - 1],
            device_id={"tok": lax.rem(t + step, n_tok)},
            device_id_type=MESH,
        )
        copy.start()
        pending.append(copy)
        kv_copies.append(copy)

    state_all[z] = state_ref[z * heads_dev // group].astype(jnp.bfloat16)

    def tile_loop(body):
        def one(tile, carry):
            body(pl.multiple_of(tile * row_tile, row_tile))
            return carry

        lax.fori_loop(0, tiles, one, 0)

    def read_slice(source, begin):
        shift = lax.rem(head - source * slice_rows, head)

        def one(row):
            q = q_ref[pl.ds(row, row_tile), :]
            turned = pltpu.roll(q.astype(jnp.float32), shift, 1).astype(jnp.bfloat16)
            total = None
            span = min(8, slice_rows)
            for a in range(0, slice_rows, span):
                phi = jnp.concatenate([turned[:, a + i : a + i + 1] * q for i in range(span)], axis=1)
                term = jnp.dot(
                    phi,
                    state_all[source, a * head : (a + span) * head, :],
                    preferred_element_type=jnp.float32,
                )
                total = term if total is None else total + term
            if begin:
                acc[pl.ds(row, row_tile), :] = total
            else:
                acc[pl.ds(row, row_tile), :] += total

        tile_loop(one)

    def attend(k_ref, v_ref, causal):
        def one(row):
            q = q_ref[pl.ds(row, row_tile), :]
            scores = lax.dot_general(
                q, k_ref[...], (((1,), (1,)), ((), ())), preferred_element_type=jnp.float32
            )
            weights = scores * scores
            if causal:
                place = row + lax.broadcasted_iota(jnp.int32, (row_tile, keys), 0)
                key = lax.broadcasted_iota(jnp.int32, (row_tile, keys), 1)
                weights = jnp.where(key * heads_dev <= place, weights, 0.0)
            acc[pl.ds(row, row_tile), :] += jnp.dot(
                weights.astype(jnp.bfloat16), v_ref[...], preferred_element_type=jnp.float32
            )

        tile_loop(one)

    forwards = {}

    def forward(step, source, stage):
        count = 2 ** stage
        for i in range(count):
            held = t
            for j in range(stage):
                if (i >> j) % 2:
                    held = flip(held, bits[j])
            where = state_all.at[source, pl.ds(pl.multiple_of(held * piece, piece), piece), :]
            slot = (step - 1) * (n_tok - 1) + count - 1 + i
            copy = pltpu.make_async_remote_copy(
                src_ref=where,
                dst_ref=where,
                send_sem=f_send.at[slot],
                recv_sem=f_recv.at[slot],
                device_id={"tok": flip(t, bits[stage])},
                device_id_type=MESH,
            )
            copy.start()
            pending.append(copy)
            forwards.setdefault((step, stage), []).append(copy)

    read_slice(z, True)
    stages = len(bits)
    for tick in range(n_feat - 1 + stages):
        if tick == min(1, n_feat - 2 + stages):
            attend(kv_ref.at[0], kv_ref.at[1], True)
        if tick == min(2, n_feat - 2 + stages):
            for copy in kv_copies:
                copy.wait_recv()

            def far(block, carry):
                attend(kv_all.at[block, 0], kv_all.at[block, 1], False)
                return carry

            lax.fori_loop(0, t, far, 0)
        ready = []
        for step in range(1, n_feat):
            stage = tick - (step - 1)
            source = lax.rem(z - step + n_feat, n_feat)
            if stage < 0 or stage > stages:
                continue
            if stage == 0:
                z_copies[step - 1].wait_recv()
            else:
                for copy in forwards[(step, stage - 1)]:
                    copy.wait_recv()
            if stage < stages:
                forward(step, source, stage)
            else:
                ready.append(source)
        for source in ready:
            read_slice(source, False)

    def finish(row):
        summed = acc[pl.ds(row, row_tile), :]
        mean_square = jnp.mean(summed * summed, axis=-1, keepdims=True)
        out_ref[pl.ds(row, row_tile), :] = (
            summed * lax.rsqrt(mean_square + 1e-06) * gain_ref[...]
        ).astype(jnp.bfloat16)

    tile_loop(finish)
    for copy in pending:
        copy.wait_send()


def local(query_matrix_rows, key_matrix_rows, value_rows, incoming_state, out_gain):
    tok_len, heads_dev, head = query_matrix_rows.shape
    n_feat = lax.axis_size("feat")
    n_tok = lax.axis_size("tok")
    kv_heads, slice_len, _ = incoming_state.shape
    rows = tok_len * heads_dev
    own = lax.axis_index("feat") * heads_dev // (QUERY_HEAD_COUNT // KEY_VALUE_HEADS)
    kv = jnp.stack(
        [
            lax.dynamic_index_in_dim(key_matrix_rows, own, 1, keepdims=False),
            lax.dynamic_index_in_dim(value_rows, own, 1, keepdims=False),
        ]
    )
    row_tile = min(512, rows)
    vmem = pl.BlockSpec(memory_space=pltpu.VMEM)
    out = pl.pallas_call(
        functools.partial(kernel, n_feat, n_tok, heads_dev, row_tile),
        out_shape=jax.ShapeDtypeStruct((rows, head), jnp.bfloat16),
        in_specs=[vmem] * 4,
        out_specs=vmem,
        scratch_shapes=[
            pltpu.VMEM((n_feat, slice_len, head), jnp.bfloat16),
            pltpu.VMEM((kv_heads, slice_len // n_tok, head), jnp.bfloat16),
            pltpu.VMEM((n_tok, 2, tok_len, head), jnp.bfloat16),
            pltpu.VMEM((rows, head), jnp.float32),
            pltpu.SemaphoreType.DMA((n_feat - 1,)),
            pltpu.SemaphoreType.DMA((n_feat - 1,)),
            pltpu.SemaphoreType.DMA(((n_feat - 1) * (n_tok - 1),)),
            pltpu.SemaphoreType.DMA(((n_feat - 1) * (n_tok - 1),)),
            pltpu.SemaphoreType.DMA((n_tok - 1,)),
            pltpu.SemaphoreType.DMA((n_tok - 1,)),
        ],
        compiler_params=pltpu.CompilerParams(
            collective_id=0, has_side_effects=True, vmem_limit_bytes=40 * 2**20
        ),
    )(query_matrix_rows.reshape(rows, head), kv, incoming_state, out_gain.reshape(1, head))
    return out.reshape(tok_len, heads_dev, head)


def solution(mesh):
    return jax.shard_map(
        local,
        mesh=mesh,
        in_specs=(
            P(("grp", "tok"), "feat", None),
            P(("grp", "tok"), None, None),
            P(("grp", "tok"), None, None),
            P("grp", "feat", None),
            P(),
        ),
        out_specs=P(("grp", "tok"), "feat", None),
        check_vma=False,
    )
```

```python
import functools

import jax
import jax.numpy as jnp
from jax import lax
from jax.experimental import pallas as pl
from jax.experimental.pallas import tpu as pltpu
from jax.sharding import PartitionSpec as P

QUERY_HEAD_COUNT = 32
KEY_VALUE_HEADS = 2
MESH = pl.DeviceIdType.MESH


def flip(place, bit):
    return place + bit - 2 * bit * ((place // bit) % 2)


def kernel(
    n_feat, n_tok, heads_dev, row_tile, cuts,
    q_ref, kv_ref, state_ref, gain_ref, out_ref,
    state_all, send_wide, send_buf, own_wide, kv_all, acc,
    in_sem, z_send, z_recv, f_send, f_recv, kv_send, kv_recv,
):
    z = lax.axis_index("feat")
    t = lax.axis_index("tok")
    group = QUERY_HEAD_COUNT // KEY_VALUE_HEADS
    rows, head = q_ref.shape
    slice_len = state_all.shape[1]
    slice_rows = slice_len // head
    tiles = rows // row_tile
    piece = slice_len // n_tok
    cut = piece // cuts
    unit = max(1, tiles // 2)
    keys = kv_ref.shape[1]
    bits = []
    while 2 ** len(bits) < n_tok:
        bits.append(n_tok // 2 ** (len(bits) + 1))

    first = pl.multiple_of(t * piece, piece)
    own = z * heads_dev // group
    members = group // heads_dev
    for g in range(KEY_VALUE_HEADS):
        pltpu.make_async_copy(
            state_ref.at[g, pl.ds(first, piece), :], send_wide.at[g], in_sem.at[g]
        ).start()
    own_copy = pltpu.make_async_copy(state_ref.at[own], own_wide, in_sem.at[KEY_VALUE_HEADS])
    own_copy.start()

    barrier = pltpu.get_barrier_semaphore()
    for step in range(1, n_feat):
        pl.semaphore_signal(
            barrier, inc=1, device_id={"feat": lax.rem(z + step, n_feat)}, device_id_type=MESH
        )
    for step in range(1, n_tok):
        pl.semaphore_signal(
            barrier, inc=1, device_id={"tok": lax.rem(t + step, n_tok)}, device_id_type=MESH
        )

    for g in range(KEY_VALUE_HEADS):
        pltpu.make_async_copy(
            state_ref.at[g, pl.ds(first, piece), :], send_wide.at[g], in_sem.at[g]
        ).wait()
        send_buf[g] = send_wide[g].astype(jnp.bfloat16)

    pl.semaphore_wait(barrier, n_feat + n_tok - 2)

    pending = []

    def along(source, c, src_ref, sem, peer):
        return pltpu.make_async_remote_copy(
            src_ref=src_ref,
            dst_ref=state_all.at[source, pl.ds(first + c * cut, cut), :],
            send_sem=sem,
            recv_sem=z_recv.at[source * cuts + c],
            device_id={"feat": peer},
            device_id_type=MESH,
        )

    for c in range(cuts):
        piece_of = lambda g: send_buf.at[g, pl.ds(c * cut, cut), :]
        for step in range(1, n_feat):
            peer = lax.rem(z + step, n_feat)
            copy = along(z, c, piece_of(peer // members), z_send.at[(step - 1) * cuts + c], peer)
            copy.start()
            pending.append(copy)
    upper = 2 * z >= n_feat
    mirrored = jnp.where(upper, n_feat - 1 - z, z)

    def source_of(step):
        near = jnp.where(step - 1 < mirrored, step - 1, step)
        return jnp.where(upper, n_feat - 1 - near, near)

    def pass_on(step, c):
        source = source_of(step)
        here = state_all.at[source, pl.ds(first + c * cut, cut), :]
        along(source, c, here, z_send.at[(step - 1) * cuts + c], source).wait_recv()

    kv_copies = []
    for step in range(1, n_tok):
        copy = pltpu.make_async_remote_copy(
            src_ref=kv_ref,
            dst_ref=kv_all.at[t],
            send_sem=kv_send.at[step - 1],
            recv_sem=kv_recv.at[step - 1],
            device_id={"tok": lax.rem(t + step, n_tok)},
            device_id_type=MESH,
        )
        copy.start()
        pending.append(copy)
        kv_copies.append(copy)

    own_copy.wait()
    state_all[z] = own_wide[...].astype(jnp.bfloat16)

    def tile_loop(body, begin=0, end=tiles):
        def one(tile, carry):
            body(pl.multiple_of(tile * row_tile, row_tile))
            return carry

        lax.fori_loop(begin, end, one, 0)

    def read_slice(source, begin, tile, count):
        shift = lax.rem(head - source * slice_rows, head)

        def one(row):
            q = q_ref[pl.ds(row, row_tile), :]
            turned = pltpu.roll(q.astype(jnp.float32), shift, 1).astype(jnp.bfloat16)
            total = None
            span = min(32, slice_rows)
            for a in range(0, slice_rows, span):
                phi = jnp.concatenate([turned[:, a + i : a + i + 1] * q for i in range(span)], axis=1)
                term = jnp.dot(
                    phi,
                    state_all[source, a * head : (a + span) * head, :],
                    preferred_element_type=jnp.float32,
                )
                total = term if total is None else total + term
            if begin:
                acc[pl.ds(row, row_tile), :] = total
            else:
                acc[pl.ds(row, row_tile), :] += total

        tile_loop(one, tile, tile + count)

    def attend(k_ref, v_ref, causal):
        def one(row):
            q = q_ref[pl.ds(row, row_tile), :]
            scores = lax.dot_general(
                q, k_ref[...], (((1,), (1,)), ((), ())), preferred_element_type=jnp.float32
            )
            weights = scores * scores
            if causal:
                place = row + lax.broadcasted_iota(jnp.int32, (row_tile, keys), 0)
                key = lax.broadcasted_iota(jnp.int32, (row_tile, keys), 1)
                weights = jnp.where(key * heads_dev <= place, weights, 0.0)
            acc[pl.ds(row, row_tile), :] += jnp.dot(
                weights.astype(jnp.bfloat16), v_ref[...], preferred_element_type=jnp.float32
            )

        tile_loop(one)

    forwards = {}

    def forward(item, source, c, stage):
        count = 2 ** stage
        for i in range(count):
            held = t
            for j in range(stage):
                if (i >> j) % 2:
                    held = flip(held, bits[j])
            where = state_all.at[source, pl.ds(pl.multiple_of(held * piece + c * cut, cut), cut), :]
            slot = item * (n_tok - 1) + count - 1 + i
            copy = pltpu.make_async_remote_copy(
                src_ref=where,
                dst_ref=where,
                send_sem=f_send.at[slot],
                recv_sem=f_recv.at[slot],
                device_id={"tok": flip(t, bits[stage])},
                device_id_type=MESH,
            )
            copy.start()
            pending.append(copy)
            forwards.setdefault((item, stage), []).append(copy)

    def earlier_blocks():
        for copy in kv_copies:
            copy.wait_recv()

        def far(block, carry):
            attend(kv_all.at[block, 0], kv_all.at[block, 1], False)
            return carry

        lax.fori_loop(0, t, far, 0)

    def own_block():
        attend(kv_ref.at[0], kv_ref.at[1], True)

    work = [functools.partial(read_slice, z, True, tile, unit) for tile in range(0, tiles, unit)]
    work += [own_block, earlier_blocks]
    stages = len(bits)
    items = [(step, c) for step in range(1, n_feat) for c in range(cuts)]
    for tick in range(len(items) + stages):
        if work:
            work.pop(0)()
        for stage in range(stages + 1):
            item = tick - stage
            if item < 0 or item >= len(items):
                continue
            step, c = items[item]
            source = source_of(step)
            if stage == 0:
                pass_on(step, c)
            else:
                for copy in forwards[(item, stage - 1)]:
                    copy.wait_recv()
            if stage < stages:
                forward(item, source, c, stage)
            elif c == cuts - 1:
                work += [
                    functools.partial(read_slice, source, False, tile, unit)
                    for tile in range(0, tiles, unit)
                ]
    for piece_of_work in work:
        piece_of_work()

    def finish(row):
        summed = acc[pl.ds(row, row_tile), :]
        mean_square = jnp.mean(summed * summed, axis=-1, keepdims=True)
        out_ref[pl.ds(row, row_tile), :] = (
            summed * lax.rsqrt(mean_square + 1e-06) * gain_ref[...]
        ).astype(jnp.bfloat16)

    tile_loop(finish)
    for copy in pending:
        copy.wait_send()


def local(query_matrix_rows, key_matrix_rows, value_rows, incoming_state, out_gain):
    tok_len, heads_dev, head = query_matrix_rows.shape
    n_feat = lax.axis_size("feat")
    n_tok = lax.axis_size("tok")
    kv_heads, slice_len, _ = incoming_state.shape
    rows = tok_len * heads_dev
    own = lax.axis_index("feat") * heads_dev // (QUERY_HEAD_COUNT // KEY_VALUE_HEADS)
    kv = jnp.stack(
        [
            lax.dynamic_index_in_dim(key_matrix_rows, own, 1, keepdims=False),
            lax.dynamic_index_in_dim(value_rows, own, 1, keepdims=False),
        ]
    )
    row_tile = min(512, rows)
    cuts = max(1, 32 // (n_feat * n_tok))
    vmem = pl.BlockSpec(memory_space=pltpu.VMEM)
    out = pl.pallas_call(
        functools.partial(kernel, n_feat, n_tok, heads_dev, row_tile, cuts),
        out_shape=jax.ShapeDtypeStruct((rows, head), jnp.bfloat16),
        in_specs=[vmem, vmem, pl.BlockSpec(memory_space=pltpu.HBM), vmem],
        out_specs=vmem,
        scratch_shapes=[
            pltpu.VMEM((n_feat, slice_len, head), jnp.bfloat16),
            pltpu.VMEM((kv_heads, slice_len // n_tok, head), jnp.float32),
            pltpu.VMEM((kv_heads, slice_len // n_tok, head), jnp.bfloat16),
            pltpu.VMEM((slice_len, head), jnp.float32),
            pltpu.VMEM((n_tok, 2, tok_len, head), jnp.bfloat16),
            pltpu.VMEM((rows, head), jnp.float32),
            pltpu.SemaphoreType.DMA((kv_heads + 1,)),
            pltpu.SemaphoreType.DMA(((n_feat - 1) * cuts,)),
            pltpu.SemaphoreType.DMA((n_feat * cuts,)),
            pltpu.SemaphoreType.DMA(((n_feat - 1) * (n_tok - 1) * cuts,)),
            pltpu.SemaphoreType.DMA(((n_feat - 1) * (n_tok - 1) * cuts,)),
            pltpu.SemaphoreType.DMA((n_tok - 1,)),
            pltpu.SemaphoreType.DMA((n_tok - 1,)),
        ],
        compiler_params=pltpu.CompilerParams(
            collective_id=0, has_side_effects=True, vmem_limit_bytes=40 * 2**20
        ),
    )(query_matrix_rows.reshape(rows, head), kv, incoming_state, out_gain.reshape(1, head))
    return out.reshape(tok_len, heads_dev, head)


def solution(mesh):
    return jax.shard_map(
        local,
        mesh=mesh,
        in_specs=(
            P(("grp", "tok"), "feat", None),
            P(("grp", "tok"), None, None),
            P(("grp", "tok"), None, None),
            P("grp", "feat", None),
            P(),
        ),
        out_specs=P(("grp", "tok"), "feat", None),
        check_vma=False,
    )
```

```python
import functools

import jax
import jax.numpy as jnp
from jax import lax
from jax.experimental import pallas as pl
from jax.experimental.pallas import tpu as pltpu
from jax.sharding import PartitionSpec as P

QUERY_HEAD_COUNT = 32
KEY_VALUE_HEADS = 2
MESH = pl.DeviceIdType.MESH


def flip(place, bit):
    return place + bit - 2 * bit * ((place // bit) % 2)


def kernel(
    n_feat, n_tok, heads_dev, row_tile, cuts,
    q_ref, kv_ref, state_ref, gain_ref, out_ref,
    state_all, send_wide, send_buf, own_wide, kv_all, acc,
    in_sem, z_send, z_recv, f_send, f_recv, kv_send, kv_recv,
):
    z = lax.axis_index("feat")
    t = lax.axis_index("tok")
    group = QUERY_HEAD_COUNT // KEY_VALUE_HEADS
    rows, head = q_ref.shape
    slice_len = state_all.shape[1]
    slice_rows = slice_len // head
    tiles = rows // row_tile
    piece = slice_len // n_tok
    cut = piece // cuts
    unit = max(1, tiles // 2)
    keys = kv_ref.shape[1]
    bits = []
    while 2 ** len(bits) < n_tok:
        bits.append(n_tok // 2 ** (len(bits) + 1))

    first = pl.multiple_of(t * piece, piece)
    own = z * heads_dev // group
    members = group // heads_dev
    for g in range(KEY_VALUE_HEADS):
        pltpu.make_async_copy(
            state_ref.at[g, pl.ds(first, piece), :], send_wide.at[g], in_sem.at[g]
        ).start()
    own_copy = pltpu.make_async_copy(state_ref.at[own], own_wide, in_sem.at[KEY_VALUE_HEADS])
    own_copy.start()

    barrier = pltpu.get_barrier_semaphore()
    for step in range(1, n_feat):
        pl.semaphore_signal(
            barrier, inc=1, device_id={"feat": lax.rem(z + step, n_feat)}, device_id_type=MESH
        )
    for step in range(1, n_tok):
        pl.semaphore_signal(
            barrier, inc=1, device_id={"tok": lax.rem(t + step, n_tok)}, device_id_type=MESH
        )

    for g in range(KEY_VALUE_HEADS):
        pltpu.make_async_copy(
            state_ref.at[g, pl.ds(first, piece), :], send_wide.at[g], in_sem.at[g]
        ).wait()
        send_buf[g] = send_wide[g].astype(jnp.bfloat16)

    pl.semaphore_wait(barrier, n_feat + n_tok - 2)

    pending = []

    def along(source, c, src_ref, sem, peer):
        return pltpu.make_async_remote_copy(
            src_ref=src_ref,
            dst_ref=state_all.at[source, pl.ds(first + c * cut, cut), :],
            send_sem=sem,
            recv_sem=z_recv.at[source * cuts + c],
            device_id={"feat": peer},
            device_id_type=MESH,
        )

    for c in range(cuts):
        piece_of = lambda g: send_buf.at[g, pl.ds(c * cut, cut), :]
        for step in range(1, n_feat):
            peer = lax.rem(z + step, n_feat)
            copy = along(z, c, piece_of(peer // members), z_send.at[(step - 1) * cuts + c], peer)
            copy.start()
            pending.append(copy)
    upper = 2 * z >= n_feat
    mirrored = jnp.where(upper, n_feat - 1 - z, z)

    def source_of(step):
        near = jnp.where(step - 1 < mirrored, step - 1, step)
        return jnp.where(upper, n_feat - 1 - near, near)

    def pass_on(step, c):
        source = source_of(step)
        here = state_all.at[source, pl.ds(first + c * cut, cut), :]
        along(source, c, here, z_send.at[(step - 1) * cuts + c], source).wait_recv()

    kv_copies = []
    for step in range(1, n_tok):
        copy = pltpu.make_async_remote_copy(
            src_ref=kv_ref,
            dst_ref=kv_all.at[t],
            send_sem=kv_send.at[step - 1],
            recv_sem=kv_recv.at[step - 1],
            device_id={"tok": lax.rem(t + step, n_tok)},
            device_id_type=MESH,
        )
        pl.when(t + step < n_tok)(copy.start)
        kv_copies.append(copy)

    own_copy.wait()
    state_all[z] = own_wide[...].astype(jnp.bfloat16)

    def tile_loop(body, begin=0, end=tiles):
        def one(tile, carry):
            body(pl.multiple_of(tile * row_tile, row_tile))
            return carry

        lax.fori_loop(begin, end, one, 0)

    def read_slice(source, begin, tile, count):
        shift = lax.rem(head - source * slice_rows, head)

        def one(row):
            q = q_ref[pl.ds(row, row_tile), :]
            turned = pltpu.roll(q.astype(jnp.float32), shift, 1).astype(jnp.bfloat16)
            total = None
            span = min(32, slice_rows)
            for a in range(0, slice_rows, span):
                phi = jnp.concatenate([turned[:, a + i : a + i + 1] * q for i in range(span)], axis=1)
                term = jnp.dot(
                    phi,
                    state_all[source, a * head : (a + span) * head, :],
                    preferred_element_type=jnp.float32,
                )
                total = term if total is None else total + term
            if begin:
                acc[pl.ds(row, row_tile), :] = total
            else:
                acc[pl.ds(row, row_tile), :] += total

        tile_loop(one, tile, tile + count)

    def attend(k_ref, v_ref, causal):
        def one(row):
            q = q_ref[pl.ds(row, row_tile), :]
            scores = lax.dot_general(
                q, k_ref[...], (((1,), (1,)), ((), ())), preferred_element_type=jnp.float32
            )
            weights = scores * scores
            if causal:
                place = row + lax.broadcasted_iota(jnp.int32, (row_tile, keys), 0)
                key = lax.broadcasted_iota(jnp.int32, (row_tile, keys), 1)
                weights = jnp.where(key * heads_dev <= place, weights, 0.0)
            acc[pl.ds(row, row_tile), :] += jnp.dot(
                weights.astype(jnp.bfloat16), v_ref[...], preferred_element_type=jnp.float32
            )

        tile_loop(one)

    forwards = {}

    def forward(item, source, c, stage):
        count = 2 ** stage
        for i in range(count):
            held = t
            for j in range(stage):
                if (i >> j) % 2:
                    held = flip(held, bits[j])
            where = state_all.at[source, pl.ds(pl.multiple_of(held * piece + c * cut, cut), cut), :]
            slot = item * (n_tok - 1) + count - 1 + i
            copy = pltpu.make_async_remote_copy(
                src_ref=where,
                dst_ref=where,
                send_sem=f_send.at[slot],
                recv_sem=f_recv.at[slot],
                device_id={"tok": flip(t, bits[stage])},
                device_id_type=MESH,
            )
            copy.start()
            pending.append(copy)
            forwards.setdefault((item, stage), []).append(copy)

    def earlier_blocks():
        for step, copy in enumerate(kv_copies, 1):
            pl.when(t >= step)(copy.wait_recv)

        def far(block, carry):
            attend(kv_all.at[block, 0], kv_all.at[block, 1], False)
            return carry

        lax.fori_loop(0, t, far, 0)

    def own_block():
        attend(kv_ref.at[0], kv_ref.at[1], True)

    work = [functools.partial(read_slice, z, True, tile, unit) for tile in range(0, tiles, unit)]
    work += [own_block, earlier_blocks]
    stages = len(bits)
    items = [(step, c) for step in range(1, n_feat) for c in range(cuts)]
    for tick in range(len(items) + stages):
        if work:
            work.pop(0)()
        for stage in range(stages + 1):
            item = tick - stage
            if item < 0 or item >= len(items):
                continue
            step, c = items[item]
            source = source_of(step)
            if stage == 0:
                pass_on(step, c)
            else:
                for copy in forwards[(item, stage - 1)]:
                    copy.wait_recv()
            if stage < stages:
                forward(item, source, c, stage)
            elif c == cuts - 1:
                work += [
                    functools.partial(read_slice, source, False, tile, unit)
                    for tile in range(0, tiles, unit)
                ]
    for piece_of_work in work:
        piece_of_work()

    def finish(row):
        summed = acc[pl.ds(row, row_tile), :]
        mean_square = jnp.mean(summed * summed, axis=-1, keepdims=True)
        out_ref[pl.ds(row, row_tile), :] = (
            summed * lax.rsqrt(mean_square + 1e-06) * gain_ref[...]
        ).astype(jnp.bfloat16)

    tile_loop(finish)
    for copy in pending:
        copy.wait_send()
    for step, copy in enumerate(kv_copies, 1):
        pl.when(t + step < n_tok)(copy.wait_send)


def local(query_matrix_rows, key_matrix_rows, value_rows, incoming_state, out_gain):
    tok_len, heads_dev, head = query_matrix_rows.shape
    n_feat = lax.axis_size("feat")
    n_tok = lax.axis_size("tok")
    kv_heads, slice_len, _ = incoming_state.shape
    rows = tok_len * heads_dev
    own = lax.axis_index("feat") * heads_dev // (QUERY_HEAD_COUNT // KEY_VALUE_HEADS)
    kv = jnp.stack(
        [
            lax.dynamic_index_in_dim(key_matrix_rows, own, 1, keepdims=False),
            lax.dynamic_index_in_dim(value_rows, own, 1, keepdims=False),
        ]
    )
    row_tile = min(512, rows)
    cuts = max(1, 32 // (n_feat * n_tok))
    vmem = pl.BlockSpec(memory_space=pltpu.VMEM)
    out = pl.pallas_call(
        functools.partial(kernel, n_feat, n_tok, heads_dev, row_tile, cuts),
        out_shape=jax.ShapeDtypeStruct((rows, head), jnp.bfloat16),
        in_specs=[vmem, vmem, pl.BlockSpec(memory_space=pltpu.HBM), vmem],
        out_specs=vmem,
        scratch_shapes=[
            pltpu.VMEM((n_feat, slice_len, head), jnp.bfloat16),
            pltpu.VMEM((kv_heads, slice_len // n_tok, head), jnp.float32),
            pltpu.VMEM((kv_heads, slice_len // n_tok, head), jnp.bfloat16),
            pltpu.VMEM((slice_len, head), jnp.float32),
            pltpu.VMEM((n_tok, 2, tok_len, head), jnp.bfloat16),
            pltpu.VMEM((rows, head), jnp.float32),
            pltpu.SemaphoreType.DMA((kv_heads + 1,)),
            pltpu.SemaphoreType.DMA(((n_feat - 1) * cuts,)),
            pltpu.SemaphoreType.DMA((n_feat * cuts,)),
            pltpu.SemaphoreType.DMA(((n_feat - 1) * (n_tok - 1) * cuts,)),
            pltpu.SemaphoreType.DMA(((n_feat - 1) * (n_tok - 1) * cuts,)),
            pltpu.SemaphoreType.DMA((n_tok - 1,)),
            pltpu.SemaphoreType.DMA((n_tok - 1,)),
        ],
        compiler_params=pltpu.CompilerParams(
            collective_id=0, has_side_effects=True, vmem_limit_bytes=40 * 2**20
        ),
    )(query_matrix_rows.reshape(rows, head), kv, incoming_state, out_gain.reshape(1, head))
    return out.reshape(tok_len, heads_dev, head)


def solution(mesh):
    return jax.shard_map(
        local,
        mesh=mesh,
        in_specs=(
            P(("grp", "tok"), "feat", None),
            P(("grp", "tok"), None, None),
            P(("grp", "tok"), None, None),
            P("grp", "feat", None),
            P(),
        ),
        out_specs=P(("grp", "tok"), "feat", None),
        check_vma=False,
    )
```
